32 devices in a mesh: grp: 4 (over z), shard: 8 (over y, x, core).
Axes of the slice: x: 2, y: 2, z: 4, core: 2. Of those that a mesh axis runs over, the one named last changes fastest.
Arguments:
- activations: bfloat16 [256, 5120], P('grp', 'shard'), may hold values from -6 to 6
- grad_outputs: bfloat16 [256, 27648], P('shard', 'grp'), may hold values from -6 to 6
- basis_in: bfloat16 [5120, 2560], P('shard', 'grp'), may hold values from -0.078125 to 0.078125
- basis_out: bfloat16 [27648, 13824], P('grp', 'shard'), may hold values from -0.0390625 to 0.0390625
- query_grads: bfloat16 [4, 2560, 13824], P('grp', None, 'shard'), may hold values from -0.0009765625 to 0.0009765625
Outputs:
- scores: float32 [4, 256], P('grp', 'shard')
The draws below stay inside these ranges and needn't reach their ends.
All inputs are finite; a program needn't handle non-finite values.
Results may differ from the reference program's by a relative error of at most 0.0041.
Values may be sent and summed in bfloat16 or wider, within the bound.
A program may use at most 128 MiB of HBM per device.

```python
import jax
import jax.numpy as jnp
from jax import lax

DIN = 5120
DOUT = 27648
EIG_IN = 2560
EIG_OUT = 13824
TOKENS = 256
N_GRP = 4


def with_spikes(result, key, source, target, blocks, factor):
    owner, partner = [(jnp.arange(result.shape[position]) // (result.shape[position] // blocks)).reshape([-1 if axis == position else 1 for axis in range(result.ndim)]) for position in (source, target)]
    chosen = jax.random.permutation(key, blocks)[partner]
    strong = (owner == chosen) | (owner == (partner + blocks // 2) % blocks)
    return jnp.where(strong, factor * result, result)


def shard_levels(key, shape, pieces, least, top_value):
    gain = 1.0
    for axis_at, shards_of in pieces:
        draws = jax.random.uniform(jax.random.fold_in(jax.random.fold_in(key, 6), axis_at), (shards_of,), jnp.float32, least / len(pieces), top_value / len(pieces))
        gain = gain * jnp.repeat(jnp.exp(draws), shape[axis_at] // shards_of).reshape((-1,) + (1,) * (len(shape) - 1 - axis_at))
    return gain


def gaussian(rng, extent, deviation, reach, shards=(), dtype=jnp.bfloat16):
    drawn = jax.random.normal(rng, extent, jnp.float32) * deviation
    if len(shards) > 0:
        drawn = shard_levels(rng, extent, shards, -0.22, 0.18) * drawn
    return jnp.clip(drawn, min=-reach, max=reach).astype(dtype)


def noise_with(stream_key, shape, spread, limit, shards, heavy, dtype=jnp.bfloat16):
    drawn = spread * jax.random.normal(stream_key, shape, jnp.float32)
    if shards:
        drawn = drawn * shard_levels(stream_key, shape, shards, -0.22, 0.18)
    return jnp.clip(with_spikes(drawn, jax.random.fold_in(stream_key, 3), *heavy), -limit, limit).astype(dtype)


def setup_inputs(seed: int = 0) -> dict:
    keys = jax.random.split(jax.random.key(seed), 6)
    return {
        "activations": gaussian(keys[0], (TOKENS, DIN), 1.0, 6.0, ((0, 4), (1, 8))),
        "grad_outputs": noise_with(keys[1], (TOKENS, DOUT), 1.0, 6.0, ((0, 8), (1, 4)), (1, 0, 8, 2.0)),
        "basis_in": gaussian(keys[2], (DIN, EIG_IN), DIN ** -0.5, 0.078125, ((0, 8), (1, 4))),
        "basis_out": gaussian(keys[3], (DOUT, EIG_OUT), DOUT ** -0.5, 0.0390625, ((0, 4), (1, 8))),
        "query_grads": gaussian(keys[4], (N_GRP, EIG_IN, EIG_OUT), (EIG_IN * EIG_OUT) ** -0.5, 0.0009765625, ((0, 4), (2, 8))),
    }


def reference(activations, grad_outputs, basis_in, basis_out, query_grads):
    act_rot = jnp.dot(activations, basis_in, preferred_element_type=jnp.float32).astype(jnp.bfloat16)
    out_rot = jnp.dot(grad_outputs, basis_out, preferred_element_type=jnp.float32).astype(jnp.bfloat16)
    out_wide = out_rot.astype(jnp.float32)

    def one_query(query):
        mixed = jnp.dot(act_rot, query, preferred_element_type=jnp.float32)
        return jnp.sum(mixed * out_wide, axis=1)

    return lax.map(one_query, query_grads)
```

```python
import functools

import jax
import jax.numpy as jnp
from jax import lax
from jax.experimental import pallas as pl
from jax.experimental.pallas import tpu as pltpu
from jax.sharding import PartitionSpec as P

F32, BF16 = jnp.float32, jnp.bfloat16
ROWS = 144
SKEW = 2
NT = (((1,), (1,)), ((), ()))


def remote(src, dst, send, recv, where):
    return pltpu.make_async_remote_copy(
        src_ref=src, dst_ref=dst, send_sem=send, recv_sem=recv,
        device_id=where, device_id_type=pl.DeviceIdType.MESH,
    )


def kernel(ng, ns, act, grad, bin_hbm, bout_hbm, query_hbm, score,
           bin_v, bout, query, abuf, tsend, tland, piece, arow, afull, gbuf,
           mixed, own, from_left, from_right, to_right, to_left, psend, pland,
           lsem, a_s, a_r, t_s, t_r, p_s, p_r, f_s, f_r, g_s, g_r,
           zr_s, zr_r, zl_s, zl_r, s_s, s_r):
    g, s = lax.axis_index("grp"), lax.axis_index("shard")
    chips = ns // 2
    chip, core = s // 2, s % 2
    sib = chip * 2 + 1 - core
    nch = own.shape[0]
    tok, width = abuf.shape[0] * abuf.shape[1], bin_v.shape[1]

    local = [
        pltpu.make_async_copy(bin_hbm, bin_v, lsem.at[0]),
        pltpu.make_async_copy(act, abuf.at[g], lsem.at[1]),
        pltpu.make_async_copy(grad, gbuf.at[s], lsem.at[2]),
        pltpu.make_async_copy(bout_hbm, bout, lsem.at[3]),
        pltpu.make_async_copy(query_hbm, query, lsem.at[4]),
    ]
    for copy in local:
        copy.start()

    barrier = pltpu.get_barrier_semaphore()
    for i in range(1, ns):
        pl.semaphore_signal(barrier, inc=1, device_id=(g, lax.rem(s + i, ns)),
                            device_id_type=pl.DeviceIdType.MESH)
    for i in range(1, ng):
        pl.semaphore_signal(barrier, inc=1, device_id=(lax.rem(g + i, ng), s),
                            device_id_type=pl.DeviceIdType.MESH)
    pl.semaphore_wait(barrier, ns - 1 + ng - 1)

    sends = []

    def go(copy):
        copy.start()
        sends.append(copy)

    def gather_start(src, buf, snd, rcv):
        for d in range(1, chips):
            to = lax.rem(chip + d, chips) * 2 + core
            go(remote(src, buf.at[s], snd.at[d], rcv.at[s], (g, to)))
        go(remote(src, buf.at[s], snd.at[0], rcv.at[s], (g, sib)))

    def gather_relay(buf, snd, rcv):
        for d in range(1, chips):
            k = lax.rem(chip + chips - d, chips) * 2 + core
            remote(buf.at[k], buf.at[k], snd.at[0], rcv.at[k], (g, sib)).wait_recv()
            go(remote(buf.at[k], buf.at[k], snd.at[chips + d - 1], rcv.at[k], (g, sib)))

    def gather_end(buf, snd, rcv):
        for d in range(chips):
            k = lax.rem(chip + chips - d, chips) * 2 + 1 - core
            remote(buf.at[k], buf.at[k], snd.at[0], rcv.at[k], (g, sib)).wait_recv()

    for i in range(1, ng):
        go(remote(act, abuf.at[g], a_s.at[i], a_r.at[g], (lax.rem(g + i, ng), s)))
    gather_start(grad, gbuf, g_s, g_r)

    local[0].wait()
    local[1].wait()
    for i in range(1, ng):
        k = lax.rem(g + ng - i, ng)
        remote(act, abuf.at[k], a_s.at[i], a_r.at[k], (k, s)).wait_recv()
    terms = jnp.dot(abuf[...].reshape(tok, -1), bin_v[...], preferred_element_type=F32)
    tsend[...] = terms.reshape(tsend.shape)
    for i in range(1, ns):
        k = lax.rem(s + i, ns)
        go(remote(tsend.at[k], tland.at[s], t_s.at[i], t_r.at[s], (g, k)))
    gather_relay(gbuf, g_s, g_r)
    total = tsend[s]
    for i in range(1, ns):
        k = lax.rem(s + ns - i, ns)
        remote(tsend.at[k], tland.at[k], t_s.at[i], t_r.at[k], (g, k)).wait_recv()
        total = total + tland[k]
    piece[g] = total.astype(BF16)
    for i in range(1, ng):
        go(remote(piece.at[g], piece.at[g], p_s.at[i], p_r.at[g], (lax.rem(g + i, ng), s)))
    gather_end(gbuf, g_s, g_r)
    for copy in local[2:]:
        copy.wait()

    def right(c, where):
        return remote(to_right.at[c], from_left.at[c], zr_s.at[c], zr_r.at[c], (where, s))

    def left(c, where):
        return remote(to_left.at[c], from_right.at[c], zl_s.at[c], zl_r.at[c], (where, s))

    def exchange(k):
        cr = k - SKEW * g

        @pl.when((cr >= 0) & (cr < nch))
        def _():
            @pl.when(g > 0)
            def _():
                right(cr, g).wait_recv()

            @pl.when((g > 0) & (g < ng - 1))
            def _():
                to_right[cr] = (own[cr] + from_left[cr].astype(F32)).astype(BF16)
                right(cr, g + 1).start()

            @pl.when(g == 0)
            def _():
                to_right[cr] = own[cr].astype(BF16)
                right(cr, g + 1).start()

        cl = k - SKEW * (ng - 1 - g)

        @pl.when((cl >= 0) & (cl < nch))
        def _():
            @pl.when(g < ng - 1)
            def _():
                left(cl, g).wait_recv()

            @pl.when((g < ng - 1) & (g > 0))
            def _():
                to_left[cl] = (own[cl] + from_right[cl].astype(F32)).astype(BF16)
                left(cl, g - 1).start()

            @pl.when(g == ng - 1)
            def _():
                to_left[cl] = own[cl].astype(BF16)
                left(cl, g - 1).start()

    def head(k, carry):
        rows = pl.ds(pl.multiple_of(k * ROWS, ROWS), ROWS)
        own[k] = lax.dot_general(
            bout[rows, :], gbuf[...].reshape(tok, -1), NT, preferred_element_type=F32)
        exchange(k)
        return carry

    tail = SKEW * (ng - 1)
    per = -(-nch // tail)

    def rest(k, carry):
        exchange(nch + k)

        def mix(i, carry):
            @pl.when(i < nch)
            def _():
                rows = pl.ds(pl.multiple_of(i * ROWS, ROWS), ROWS)
                mixed[i] = lax.dot_general(
                    query[rows, :], afull[...].reshape(tok, -1), NT,
                    preferred_element_type=F32)

            return carry

        return lax.fori_loop(k * per, k * per + per, mix, carry)

    lax.fori_loop(0, nch // 3, head, 0)
    for i in range(1, ng):
        k = lax.rem(g + ng - i, ng)
        remote(piece.at[k], piece.at[k], p_s.at[i], p_r.at[k], (k, s)).wait_recv()
    for k in range(ng):
        arow[:, k * width:(k + 1) * width] = piece[k]
    afull[s] = arow[...]
    gather_start(arow, afull, f_s, f_r)

    lax.fori_loop(nch // 3, 2 * nch // 3, head, 0)
    gather_relay(afull, f_s, f_r)
    lax.fori_loop(2 * nch // 3, nch, head, 0)
    gather_end(afull, f_s, f_r)
    lax.fori_loop(0, tail, rest, 0)

    def add(k, carry):
        @pl.when(g > 0)
        def _():
            own[k] = own[k] + from_left[k].astype(F32)

        @pl.when(g < ng - 1)
        def _():
            own[k] = own[k] + from_right[k].astype(F32)

        return carry + jnp.sum(mixed[k] * own[k], axis=0, keepdims=True)

    part = lax.fori_loop(0, nch, add, jnp.zeros((1, tok), F32))
    block = tok // ns
    for k in range(ns):
        psend[k] = jnp.broadcast_to(part[:, k * block:(k + 1) * block], (8, block))
    for i in range(1, ns):
        k = lax.rem(s + i, ns)
        go(remote(psend.at[k], pland.at[s], s_s.at[i], s_r.at[s], (g, k)))
    result = psend[s]
    for i in range(1, ns):
        k = lax.rem(s + ns - i, ns)
        remote(psend.at[k], pland.at[k], s_s.at[i], s_r.at[k], (g, k)).wait_recv()
        result = result + pland[k]
    score[...] = result[0:1, :]

    for copy in sends:
        copy.wait_send()

    def drain(k, carry):
        @pl.when(g < ng - 1)
        def _():
            right(k, g + 1).wait_send()

        @pl.when(g > 0)
        def _():
            left(k, g - 1).wait_send()

        return carry

    lax.fori_loop(0, nch, drain, 0)


def local(ng, ns, activations, grad_outputs, basis_in, basis_out, query_grads):
    atok, kin = activations.shape
    gtok, kout = grad_outputs.shape
    width, cols = basis_in.shape[1], basis_out.shape[1]
    eig = query_grads.shape[1]
    tok = atok * ng
    nch = cols // ROWS
    dma = pltpu.SemaphoreType.DMA
    hbm = pl.BlockSpec(memory_space=pl.ANY)
    flops = 2 * tok * (kin * width + kout * cols + eig * cols)
    return pl.pallas_call(
        functools.partial(kernel, ng, ns),
        out_shape=jax.ShapeDtypeStruct((1, gtok), F32),
        in_specs=[hbm] * 5,
        out_specs=pl.BlockSpec(memory_space=pltpu.VMEM),
        scratch_shapes=[
            pltpu.VMEM((kin, width), BF16),
            pltpu.VMEM((cols, kout), BF16),
            pltpu.VMEM((cols, eig), BF16),
            pltpu.VMEM((ng, atok, kin), BF16),
            pltpu.VMEM((ns, gtok, width), F32),
            pltpu.VMEM((ns, gtok, width), F32),
            pltpu.VMEM((ng, gtok, width), BF16),
            pltpu.VMEM((gtok, eig), BF16),
            pltpu.VMEM((ns, gtok, eig), BF16),
            pltpu.VMEM((ns, gtok, kout), BF16),
            pltpu.VMEM((nch, ROWS, tok), F32),
            pltpu.VMEM((nch, ROWS, tok), F32),
        ] + [pltpu.VMEM((nch, ROWS, tok), BF16)] * 4 + [
            pltpu.VMEM((ns, 8, gtok), F32),
            pltpu.VMEM((ns, 8, gtok), F32),
            dma((5,)),
            dma((ng,)), dma((ng,)),
            dma((ns,)), dma((ns,)),
            dma((ng,)), dma((ng,)),
            dma((ns,)), dma((ns,)),
            dma((ns,)), dma((ns,)),
            dma((nch,)), dma((nch,)), dma((nch,)), dma((nch,)),
            dma((ns,)), dma((ns,)),
        ],
        compiler_params=pltpu.CompilerParams(
            collective_id=0, has_side_effects=True, vmem_limit_bytes=60 * 2**20),
        cost_estimate=pl.CostEstimate(
            flops=flops, bytes_accessed=2 * cols * (kout + eig), transcendentals=0),
    )(activations, grad_outputs, basis_in, basis_out.T, query_grads[0].T)


def solution(mesh):
    placed = (
        P("grp", "shard"),
        P("shard", "grp"),
        P("shard", "grp"),
        P("grp", "shard"),
        P("grp", None, "shard"),
    )
    body = functools.partial(local, mesh.shape["grp"], mesh.shape["shard"])
    return jax.shard_map(
        body, mesh=mesh, in_specs=placed, out_specs=P("grp", "shard"), check_vma=False
    )
```

```python
import functools

import jax
import jax.numpy as jnp
from jax import lax
from jax.experimental import pallas as pl
from jax.experimental.pallas import tpu as pltpu
from jax.sharding import PartitionSpec as P

F32, BF16 = jnp.float32, jnp.bfloat16
ROWS = 144
SKEW = 3
NT = (((1,), (1,)), ((), ()))


def remote(src, dst, send, recv, where):
    return pltpu.make_async_remote_copy(
        src_ref=src, dst_ref=dst, send_sem=send, recv_sem=recv,
        device_id=where, device_id_type=pl.DeviceIdType.MESH,
    )


def kernel(ng, ns, act, grad, bin_hbm, bout_hbm, query_hbm, score,
           bin_v, bout, query, abuf, tsend, tland, piece, arow, afull, gbuf,
           mixed, own, from_left, from_right, to_right, to_left, psend, pland,
           lsem, a_s, a_r, t_s, t_r, p_s, p_r, f_s, f_r, g_s, g_r,
           zr_s, zr_r, zl_s, zl_r, s_s, s_r):
    g, s = lax.axis_index("grp"), lax.axis_index("shard")
    chips = ns // 2
    chip, core = s // 2, s % 2
    sib = chip * 2 + 1 - core
    nch = own.shape[0]
    tok, width = abuf.shape[0] * abuf.shape[1], bin_v.shape[1]

    local = [
        pltpu.make_async_copy(bin_hbm, bin_v, lsem.at[0]),
        pltpu.make_async_copy(act, abuf.at[g], lsem.at[1]),
        pltpu.make_async_copy(grad, gbuf.at[s], lsem.at[2]),
        pltpu.make_async_copy(bout_hbm, bout, lsem.at[3]),
        pltpu.make_async_copy(query_hbm, query, lsem.at[4]),
    ]
    for copy in local:
        copy.start()

    barrier = pltpu.get_barrier_semaphore()
    for i in range(1, ns):
        pl.semaphore_signal(barrier, inc=1, device_id=(g, lax.rem(s + i, ns)),
                            device_id_type=pl.DeviceIdType.MESH)
    for i in range(1, ng):
        pl.semaphore_signal(barrier, inc=1, device_id=(lax.rem(g + i, ng), s),
                            device_id_type=pl.DeviceIdType.MESH)
    pl.semaphore_wait(barrier, ns - 1 + ng - 1)

    sends = []

    def go(copy):
        copy.start()
        sends.append(copy)

    def gather_start(src, buf, snd, rcv):
        for d in range(1, chips):
            to = lax.rem(chip + d, chips) * 2 + core
            go(remote(src, buf.at[s], snd.at[d], rcv.at[s], (g, to)))
        go(remote(src, buf.at[s], snd.at[0], rcv.at[s], (g, sib)))

    def gather_relay(buf, snd, rcv):
        for d in range(1, chips):
            k = lax.rem(chip + chips - d, chips) * 2 + core
            remote(buf.at[k], buf.at[k], snd.at[0], rcv.at[k], (g, sib)).wait_recv()
            go(remote(buf.at[k], buf.at[k], snd.at[chips + d - 1], rcv.at[k], (g, sib)))

    def gather_end(buf, snd, rcv):
        for d in range(chips):
            k = lax.rem(chip + chips - d, chips) * 2 + 1 - core
            remote(buf.at[k], buf.at[k], snd.at[0], rcv.at[k], (g, sib)).wait_recv()

    for i in range(1, ng):
        go(remote(act, abuf.at[g], a_s.at[i], a_r.at[g], (lax.rem(g + i, ng), s)))
    gather_start(grad, gbuf, g_s, g_r)

    local[0].wait()
    local[1].wait()
    for i in range(1, ng):
        k = lax.rem(g + ng - i, ng)
        remote(act, abuf.at[k], a_s.at[i], a_r.at[k], (k, s)).wait_recv()
    terms = jnp.dot(abuf[...].reshape(tok, -1), bin_v[...], preferred_element_type=F32)
    tsend[...] = terms.reshape(tsend.shape)
    for i in range(1, ns):
        k = lax.rem(s + i, ns)
        go(remote(tsend.at[k], tland.at[s], t_s.at[i], t_r.at[s], (g, k)))
    gather_relay(gbuf, g_s, g_r)
    total = tsend[s]
    for i in range(1, ns):
        k = lax.rem(s + ns - i, ns)
        remote(tsend.at[k], tland.at[k], t_s.at[i], t_r.at[k], (g, k)).wait_recv()
        total = total + tland[k]
    piece[g] = total.astype(BF16)
    for i in range(1, ng):
        go(remote(piece.at[g], piece.at[g], p_s.at[i], p_r.at[g], (lax.rem(g + i, ng), s)))
    gather_end(gbuf, g_s, g_r)
    for copy in local[2:]:
        copy.wait()

    def right(c, where):
        return remote(to_right.at[c], from_left.at[c], zr_s.at[c], zr_r.at[c], (where, s))

    def left(c, where):
        return remote(to_left.at[c], from_right.at[c], zl_s.at[c], zl_r.at[c], (where, s))

    def exchange(k):
        cr = k - SKEW * g

        @pl.when((cr >= 0) & (cr < nch))
        def _():
            @pl.when(g > 0)
            def _():
                right(cr, g).wait_recv()

            @pl.when((g > 0) & (g < ng - 1))
            def _():
                to_right[cr] = (own[cr] + from_left[cr].astype(F32)).astype(BF16)
                right(cr, g + 1).start()

            @pl.when(g == 0)
            def _():
                to_right[cr] = own[cr].astype(BF16)
                right(cr, g + 1).start()

        cl = k - SKEW * (ng - 1 - g)

        @pl.when((cl >= 0) & (cl < nch))
        def _():
            @pl.when(g < ng - 1)
            def _():
                left(cl, g).wait_recv()

            @pl.when((g < ng - 1) & (g > 0))
            def _():
                to_left[cl] = (own[cl] + from_right[cl].astype(F32)).astype(BF16)
                left(cl, g - 1).start()

            @pl.when(g == ng - 1)
            def _():
                to_left[cl] = own[cl].astype(BF16)
                left(cl, g - 1).start()

    def head(k, carry):
        rows = pl.ds(pl.multiple_of(k * ROWS, ROWS), ROWS)
        own[k] = lax.dot_general(
            bout[rows, :], gbuf[...].reshape(tok, -1), NT, preferred_element_type=F32)
        exchange(k)
        return carry

    tail = SKEW * (ng - 1)
    per = -(-nch // tail)

    def rest(k, carry):
        exchange(nch + k)

        def mix(i, carry):
            @pl.when(i < nch)
            def _():
                rows = pl.ds(pl.multiple_of(i * ROWS, ROWS), ROWS)
                mixed[i] = lax.dot_general(
                    query[rows, :], afull[...].reshape(tok, -1), NT,
                    preferred_element_type=F32)

            return carry

        return lax.fori_loop(k * per, k * per + per, mix, carry)

    lax.fori_loop(0, nch // 3, head, 0)
    for i in range(1, ng):
        k = lax.rem(g + ng - i, ng)
        remote(piece.at[k], piece.at[k], p_s.at[i], p_r.at[k], (k, s)).wait_recv()
    for k in range(ng):
        arow[:, k * width:(k + 1) * width] = piece[k]
    afull[s] = arow[...]
    gather_start(arow, afull, f_s, f_r)

    lax.fori_loop(nch // 3, 2 * nch // 3, head, 0)
    gather_relay(afull, f_s, f_r)
    lax.fori_loop(2 * nch // 3, nch, head, 0)
    gather_end(afull, f_s, f_r)
    lax.fori_loop(0, tail, rest, 0)

    def add(k, carry):
        @pl.when(g > 0)
        def _():
            own[k] = own[k] + from_left[k].astype(F32)

        @pl.when(g < ng - 1)
        def _():
            own[k] = own[k] + from_right[k].astype(F32)

        return carry + jnp.sum(mixed[k] * own[k], axis=0, keepdims=True)

    part = lax.fori_loop(0, nch, add, jnp.zeros((1, tok), F32))
    block = tok // ns
    for k in range(ns):
        psend[k] = jnp.broadcast_to(part[:, k * block:(k + 1) * block], (8, block))
    for i in range(1, ns):
        k = lax.rem(s + i, ns)
        go(remote(psend.at[k], pland.at[s], s_s.at[i], s_r.at[s], (g, k)))
    result = psend[s]
    for i in range(1, ns):
        k = lax.rem(s + ns - i, ns)
        remote(psend.at[k], pland.at[k], s_s.at[i], s_r.at[k], (g, k)).wait_recv()
        result = result + pland[k]
    score[...] = result[0:1, :]

    for copy in sends:
        copy.wait_send()

    def drain(k, carry):
        @pl.when(g < ng - 1)
        def _():
            right(k, g + 1).wait_send()

        @pl.when(g > 0)
        def _():
            left(k, g - 1).wait_send()

        return carry

    lax.fori_loop(0, nch, drain, 0)


def local(ng, ns, activations, grad_outputs, basis_in, basis_out, query_grads):
    atok, kin = activations.shape
    gtok, kout = grad_outputs.shape
    width, cols = basis_in.shape[1], basis_out.shape[1]
    eig = query_grads.shape[1]
    tok = atok * ng
    nch = cols // ROWS
    dma = pltpu.SemaphoreType.DMA
    hbm = pl.BlockSpec(memory_space=pl.ANY)
    flops = 2 * tok * (kin * width + kout * cols + eig * cols)
    return pl.pallas_call(
        functools.partial(kernel, ng, ns),
        out_shape=jax.ShapeDtypeStruct((1, gtok), F32),
        in_specs=[hbm] * 5,
        out_specs=pl.BlockSpec(memory_space=pltpu.VMEM),
        scratch_shapes=[
            pltpu.VMEM((kin, width), BF16),
            pltpu.VMEM((cols, kout), BF16),
            pltpu.VMEM((cols, eig), BF16),
            pltpu.VMEM((ng, atok, kin), BF16),
            pltpu.VMEM((ns, gtok, width), F32),
            pltpu.VMEM((ns, gtok, width), F32),
            pltpu.VMEM((ng, gtok, width), BF16),
            pltpu.VMEM((gtok, eig), BF16),
            pltpu.VMEM((ns, gtok, eig), BF16),
            pltpu.VMEM((ns, gtok, kout), BF16),
            pltpu.VMEM((nch, ROWS, tok), F32),
            pltpu.VMEM((nch, ROWS, tok), F32),
        ] + [pltpu.VMEM((nch, ROWS, tok), BF16)] * 4 + [
            pltpu.VMEM((ns, 8, gtok), F32),
            pltpu.VMEM((ns, 8, gtok), F32),
            dma((5,)),
            dma((ng,)), dma((ng,)),
            dma((ns,)), dma((ns,)),
            dma((ng,)), dma((ng,)),
            dma((ns,)), dma((ns,)),
            dma((ns,)), dma((ns,)),
            dma((nch,)), dma((nch,)), dma((nch,)), dma((nch,)),
            dma((ns,)), dma((ns,)),
        ],
        compiler_params=pltpu.CompilerParams(
            collective_id=0, has_side_effects=True, vmem_limit_bytes=60 * 2**20),
        cost_estimate=pl.CostEstimate(
            flops=flops, bytes_accessed=2 * cols * (kout + eig), transcendentals=0),
    )(activations, grad_outputs, basis_in, basis_out.T, query_grads[0].T)


def solution(mesh):
    placed = (
        P("grp", "shard"),
        P("shard", "grp"),
        P("shard", "grp"),
        P("grp", "shard"),
        P("grp", None, "shard"),
    )
    body = functools.partial(local, mesh.shape["grp"], mesh.shape["shard"])
    return jax.shard_map(
        body, mesh=mesh, in_specs=placed, out_specs=P("grp", "shard"), check_vma=False
    )
```
